32 devices in a mesh: row: 4 (over z), col: 8 (over y, x, core).
Axes of the slice: x: 2, y: 2, z: 4, core: 2. Of those that a mesh axis runs over, the one named last changes fastest.
Arguments:
- adjusted_rows: bfloat16 [8192, 29568], P(('row', 'col')), may hold values from -5 to 5
- base_weight: bfloat16 [8192, 29568], P('row', 'col'), may hold values from -5 to 5
- range_test: bfloat16 [29568, 384], P('col'), may hold values from -0.03125 to 0.03125
- corange_test: bfloat16 [384, 8192], P(None, 'row'), may hold values from -0.0625 to 0.0625
- core_left: bfloat16 [768, 8192], P(None, 'row'), may hold values from -0.0625 to 0.0625
- core_right: bfloat16 [768, 29568], P(None, 'col'), may hold values from -1 to 1
Outputs:
- range_sketch: float32 [8192, 384], P('row')
- corange_sketch: float32 [384, 29568], P(None, 'col')
- core_solution: float32 [384, 768], P(None, 'col')
The draws below stay inside these ranges and needn't reach their ends.
All inputs are finite; a program needn't handle non-finite values.
Results may differ from the reference program's by a relative error of at most 0.0066.
Values may be sent and summed in bfloat16 or wider, within the bound.
A program may use at most 192 MiB of HBM per device.

```python
import jax
import jax.numpy as jnp
from jax import lax

R = 8192
C = 29568
K = 384
S = 768


def steps_of(rng, shape, split, smallest, top_value):
    factor_of, own = 1.0, jax.random.fold_in(rng, 6)
    for axis_at, parts in split:
        heights = jnp.exp(jax.random.uniform(jax.random.fold_in(own, axis_at), (parts,), jnp.float32, smallest / len(split), top_value / len(split)))
        factor_of = factor_of * jnp.repeat(heights, shape[axis_at] // parts).reshape([-1 if axis == axis_at else 1 for axis in range(len(shape))])
    return factor_of


def bell_draw(key, shape, width, bound, shards=(), dtype=jnp.bfloat16):
    level = steps_of(key, shape, shards, -0.22, 0.18) if shards else 1.0
    values = jax.random.normal(key, shape, jnp.float32) * width * level
    return jnp.minimum(jnp.maximum(values, -bound), bound).astype(dtype)


def setup_inputs(seed: int = 0) -> dict:
    key_of = jax.random.split(jax.random.key(seed), 7)
    adjusted_rows = bell_draw(key_of[0], (R, C), 0.7, 5.0, ((0, 32),))
    base_weight = bell_draw(key_of[1], (R, C), 0.7, 5.0, ((0, 4), (1, 8)))
    range_test = bell_draw(key_of[2], (C, K), C ** -0.5, 0.03125, ((0, 8),))
    corange_test = bell_draw(key_of[3], (K, R), R ** -0.5, 0.0625, ((1, 4),))
    core_left = bell_draw(key_of[4], (S, R), R ** -0.5, 0.0625, ((1, 4),))
    core_right = bell_draw(key_of[5], (S, C), (C // S) ** -0.5, 1.0, ((1, 8),))
    return dict(adjusted_rows=adjusted_rows, base_weight=base_weight, range_test=range_test, corange_test=corange_test, core_left=core_left, core_right=core_right)


def reference(adjusted_rows, base_weight, range_test, corange_test, core_left, core_right):
    highest = lax.Precision.HIGHEST
    difference = (adjusted_rows.astype(jnp.float32) - base_weight.astype(jnp.float32)).astype(jnp.bfloat16)
    range_sketch = jnp.dot(difference.astype(jnp.float32), range_test.astype(jnp.float32), preferred_element_type=jnp.float32)
    corange_sketch = jnp.dot(corange_test.astype(jnp.float32), difference.astype(jnp.float32), preferred_element_type=jnp.float32)
    left_product = jnp.dot(core_left.astype(jnp.float32), difference.astype(jnp.float32), preferred_element_type=jnp.float32)
    core_sketch = jnp.dot(left_product, core_right.astype(jnp.float32).T, precision=highest)
    projected = jnp.dot(core_left.astype(jnp.float32), range_sketch, precision=highest)
    gram_matrix = jnp.dot(projected.T, projected, precision=highest)
    right_hand = jnp.dot(projected.T, core_sketch, precision=highest)
    factor = jnp.linalg.cholesky(gram_matrix)
    halfway = lax.linalg.triangular_solve(factor, right_hand, left_side=True, lower=True)
    core_solution = lax.linalg.triangular_solve(factor, halfway, left_side=True, lower=True, transpose_a=True)
    return (range_sketch, corange_sketch, core_solution)
```

```python
import jax
import jax.numpy as jnp
from jax import lax
from jax.experimental import pallas as pl
from jax.experimental.pallas import tpu as pltpu
from jax.sharding import PartitionSpec as P

BLOCK = 128


def invert_block(a):
    n = a.shape[0]
    lane = lax.broadcasted_iota(jnp.int32, (1, n), 1)
    sub = lax.broadcasted_iota(jnp.int32, (n, 1), 0)
    for j in range(n):
        inv = 1.0 / a[j : j + 1, j : j + 1]
        col = a[:, j : j + 1]
        row = jnp.where(lane == j, inv, a[j : j + 1, :] * inv)
        rest = jnp.where(lane == j, 0.0, a)
        a = jnp.where(sub == j, row, rest - col * row)
    return a


def solve_kernel(gram_ref, right_ref, out_ref, work):
    k_size = gram_ref.shape[0]
    width = right_ref.shape[1]
    work[:, :k_size] = gram_ref[...]
    work[:, k_size : k_size + width] = right_ref[...]

    def step(k, carry):
        at = pl.multiple_of(k * BLOCK, BLOCK)
        inverse = invert_block(work[pl.ds(at, BLOCK), pl.ds(at, BLOCK)])
        pivot = jnp.dot(inverse, work[pl.ds(at, BLOCK), :], precision=lax.Precision.HIGHEST,
                        preferred_element_type=jnp.float32)
        column = work[:, pl.ds(at, BLOCK)]
        work[...] -= jnp.dot(column, pivot, precision=lax.Precision.HIGHEST,
                             preferred_element_type=jnp.float32)
        work[pl.ds(at, BLOCK), :] = pivot
        return carry

    lax.fori_loop(0, k_size // BLOCK, step, 0)
    out_ref[...] = work[:, k_size : k_size + width]


def solve(gram, right_hand):
    k_size, width = right_hand.shape
    padded = -(-width // 128) * 128
    right_hand = jnp.pad(right_hand, ((0, 0), (0, padded - width)))
    solved = pl.pallas_call(
        solve_kernel,
        out_shape=jax.ShapeDtypeStruct((k_size, padded), jnp.float32),
        scratch_shapes=[pltpu.VMEM((k_size, k_size + padded), jnp.float32)],
        compiler_params=pltpu.CompilerParams(vmem_limit_bytes=16 * 1024 * 1024),
    )(gram, right_hand)
    return solved[:, :width]


def local(adjusted_rows, base_weight, range_test, corange_test, core_left, core_right):
    highest = lax.Precision.HIGHEST
    f32, bf16 = jnp.float32, jnp.bfloat16
    n_col = lax.axis_size("col")
    rows = adjusted_rows.shape[0]
    width = base_weight.shape[1]
    rank = corange_test.shape[0]
    side = core_left.shape[0]
    step = 128 if rows % 128 == 0 else rows
    left_tests = jnp.concatenate([core_left, corange_test], 0).reshape(side + rank, n_col, rows)
    base_blocks = base_weight.reshape(n_col, rows, width)
    range_parts, left_sum = [], None
    for at in range(0, rows, step):
        block = adjusted_rows[at : at + step].reshape(step, n_col, width).transpose(1, 0, 2)
        block = lax.all_to_all(block, "col", split_axis=0, concat_axis=0, tiled=True)
        difference = (
            block.astype(f32) - base_blocks[:, at : at + step].astype(f32)
        ).astype(bf16).reshape(n_col * step, width)
        tests = left_tests[:, :, at : at + step].reshape(side + rank, n_col * step)
        term = jnp.dot(tests, difference, preferred_element_type=f32)
        left_sum = term if left_sum is None else left_sum + term
        range_parts.append(
            jnp.dot(difference, range_test, preferred_element_type=f32).reshape(n_col, step, rank)
        )
    left_product, corange_part = left_sum[:side], left_sum[side:]
    high = lax.reduce_precision(left_product, 8, 7)
    low = (left_product - high).astype(bf16)
    pieces = jnp.concatenate([high.astype(bf16), low], 0)
    core_two = lax.dot_general(
        pieces, core_right, (((1,), (1,)), ((), ())), preferred_element_type=f32
    )
    projected_two = jnp.dot(pieces, range_test, preferred_element_type=f32)
    both = jnp.concatenate(
        [core_two[:side] + core_two[side:], projected_two[:side] + projected_two[side:]], 1
    )
    both = lax.psum(both, ("row", "col"))
    range_part = jnp.concatenate(range_parts, 1).reshape(n_col * rows, rank)
    both, range_part, corange_part = lax.optimization_barrier(
        (both, range_part, corange_part.astype(bf16))
    )
    range_sketch = lax.psum(range_part, "col")
    corange_sketch = lax.psum(corange_part, "row").astype(f32)
    share = side // n_col
    projected = both[:, side:]
    own_columns = lax.dynamic_slice_in_dim(both, lax.axis_index("col") * share, share, 1)
    gram = jnp.dot(projected.T, projected, precision=highest)
    right_hand = jnp.dot(projected.T, own_columns, precision=highest)
    return (range_sketch, corange_sketch, solve(gram, right_hand))


def solution(mesh):
    in_specs = (
        P(("row", "col"), None),
        P("row", "col"),
        P("col", None),
        P(None, "row"),
        P(None, "row"),
        P(None, "col"),
    )
    out_specs = (P("row", None), P(None, "col"), P(None, "col"))
    return jax.shard_map(local, mesh=mesh, in_specs=in_specs, out_specs=out_specs, check_vma=False)
```

```python
import jax
import jax.numpy as jnp
from jax import lax
from jax.experimental import pallas as pl
from jax.experimental.pallas import tpu as pltpu
from jax.sharding import PartitionSpec as P

BLOCK = 128


def invert_block(a):
    n = a.shape[0]
    lane = lax.broadcasted_iota(jnp.int32, (1, n), 1)
    sub = lax.broadcasted_iota(jnp.int32, (n, 1), 0)
    for j in range(n):
        inv = 1.0 / a[j : j + 1, j : j + 1]
        col = a[:, j : j + 1]
        row = jnp.where(lane == j, inv, a[j : j + 1, :] * inv)
        rest = jnp.where(lane == j, 0.0, a)
        a = jnp.where(sub == j, row, rest - col * row)
    return a


def solve_kernel(gram_ref, right_ref, out_ref, work):
    k_size = gram_ref.shape[0]
    width = right_ref.shape[1]
    work[:, :k_size] = gram_ref[...]
    work[:, k_size : k_size + width] = right_ref[...]

    def step(k, carry):
        at = pl.multiple_of(k * BLOCK, BLOCK)
        inverse = invert_block(work[pl.ds(at, BLOCK), pl.ds(at, BLOCK)])
        pivot = jnp.dot(inverse, work[pl.ds(at, BLOCK), :], precision=lax.Precision.HIGHEST,
                        preferred_element_type=jnp.float32)
        column = work[:, pl.ds(at, BLOCK)]
        work[...] -= jnp.dot(column, pivot, precision=lax.Precision.HIGHEST,
                             preferred_element_type=jnp.float32)
        work[pl.ds(at, BLOCK), :] = pivot
        return carry

    lax.fori_loop(0, k_size // BLOCK, step, 0)
    out_ref[...] = work[:, k_size : k_size + width]


def solve(gram, right_hand):
    k_size, width = right_hand.shape
    padded = -(-width // 128) * 128
    right_hand = jnp.pad(right_hand, ((0, 0), (0, padded - width)))
    solved = pl.pallas_call(
        solve_kernel,
        out_shape=jax.ShapeDtypeStruct((k_size, padded), jnp.float32),
        scratch_shapes=[pltpu.VMEM((k_size, k_size + padded), jnp.float32)],
        compiler_params=pltpu.CompilerParams(vmem_limit_bytes=16 * 1024 * 1024),
    )(gram, right_hand)
    return solved[:, :width]


def local(adjusted_rows, base_weight, range_test, corange_test, core_left, core_right):
    highest = lax.Precision.HIGHEST
    f32, bf16 = jnp.float32, jnp.bfloat16
    n_col = lax.axis_size("col")
    rows = adjusted_rows.shape[0]
    width = base_weight.shape[1]
    rank = corange_test.shape[0]
    side = core_left.shape[0]
    step = 128 if rows % 128 == 0 else rows
    left_tests = jnp.concatenate([core_left, corange_test], 0).reshape(side + rank, n_col, rows)
    base_blocks = base_weight.reshape(n_col, rows, width)
    range_parts, left_sum = [], None
    for at in range(0, rows, step):
        block = adjusted_rows[at : at + step].reshape(step, n_col, width).transpose(1, 0, 2)
        block = lax.all_to_all(block, "col", split_axis=0, concat_axis=0, tiled=True)
        difference = (
            block.astype(f32) - base_blocks[:, at : at + step].astype(f32)
        ).astype(bf16).reshape(n_col * step, width)
        tests = left_tests[:, :, at : at + step].reshape(side + rank, n_col * step)
        term = jnp.dot(tests, difference, preferred_element_type=f32)
        left_sum = term if left_sum is None else left_sum + term
        range_parts.append(
            jnp.dot(difference, range_test, preferred_element_type=f32).reshape(n_col, step, rank)
        )
    left_product, corange_part = left_sum[:side], left_sum[side:]
    corange_sketch = lax.psum(corange_part.astype(bf16), "row").astype(f32)
    high = lax.reduce_precision(left_product, 8, 7)
    low = (left_product - high).astype(bf16)
    pieces = jnp.concatenate([high.astype(bf16), low], 0)
    core_two = lax.dot_general(
        core_right, pieces, (((1,), (1,)), ((), ())), preferred_element_type=f32
    )
    projected_two = lax.dot_general(
        range_test, pieces, (((0,), (1,)), ((), ())), preferred_element_type=f32
    )
    share, narrow = side // n_col, rank // n_col
    core_term = (core_two[:, :side] + core_two[:, side:]).reshape(n_col, share, side)
    projected_term = (projected_two[:, :side] + projected_two[:, side:]).reshape(
        n_col, narrow, side
    )
    both = jnp.concatenate([core_term, projected_term], 1)
    both = lax.all_to_all(both, "col", split_axis=0, concat_axis=0, tiled=True).sum(0)
    range_part = jnp.concatenate(range_parts, 1)
    both, range_part = lax.optimization_barrier((both, range_part.astype(bf16)))
    both = lax.psum(both, "row")
    projected = lax.all_gather(both[share:], "col", axis=0, tiled=True)
    range_own = lax.all_to_all(range_part, "col", split_axis=0, concat_axis=0, tiled=True)
    range_own = range_own.astype(f32).sum(0).astype(bf16)
    projected, range_own = lax.optimization_barrier((projected, range_own))
    range_sketch = lax.all_gather(range_own, "col", axis=0, tiled=True).astype(f32)
    gram = jnp.dot(projected, projected.T, precision=highest)
    right_hand = jnp.dot(projected, both[:share].T, precision=highest)
    return (range_sketch, corange_sketch, solve(gram, right_hand))


def solution(mesh):
    in_specs = (
        P(("row", "col"), None),
        P("row", "col"),
        P("col", None),
        P(None, "row"),
        P(None, "row"),
        P(None, "col"),
    )
    out_specs = (P("row", None), P(None, "col"), P(None, "col"))
    return jax.shard_map(local, mesh=mesh, in_specs=in_specs, out_specs=out_specs, check_vma=False)
```

```python
import jax
import jax.numpy as jnp
from jax import lax
from jax.experimental import pallas as pl
from jax.experimental.pallas import tpu as pltpu
from jax.sharding import PartitionSpec as P

BLOCK = 128


def invert_block(a):
    n = a.shape[0]
    lane = lax.broadcasted_iota(jnp.int32, (1, n), 1)
    sub = lax.broadcasted_iota(jnp.int32, (n, 1), 0)
    for j in range(n):
        inv = 1.0 / a[j : j + 1, j : j + 1]
        col = a[:, j : j + 1]
        row = jnp.where(lane == j, inv, a[j : j + 1, :] * inv)
        rest = jnp.where(lane == j, 0.0, a)
        a = jnp.where(sub == j, row, rest - col * row)
    return a


def solve_kernel(gram_ref, right_ref, out_ref, work):
    k_size = gram_ref.shape[0]
    width = right_ref.shape[1]
    work[:, :k_size] = gram_ref[...]
    work[:, k_size : k_size + width] = right_ref[...]

    def step(k, carry):
        at = pl.multiple_of(k * BLOCK, BLOCK)
        inverse = invert_block(work[pl.ds(at, BLOCK), pl.ds(at, BLOCK)])
        pivot = jnp.dot(inverse, work[pl.ds(at, BLOCK), :], precision=lax.Precision.HIGHEST,
                        preferred_element_type=jnp.float32)
        column = work[:, pl.ds(at, BLOCK)]
        work[...] -= jnp.dot(column, pivot, precision=lax.Precision.HIGHEST,
                             preferred_element_type=jnp.float32)
        work[pl.ds(at, BLOCK), :] = pivot
        return carry

    lax.fori_loop(0, k_size // BLOCK, step, 0)
    out_ref[...] = work[:, k_size : k_size + width]


def solve(gram, right_hand):
    k_size, width = right_hand.shape
    padded = -(-width // 128) * 128
    right_hand = jnp.pad(right_hand, ((0, 0), (0, padded - width)))
    solved = pl.pallas_call(
        solve_kernel,
        out_shape=jax.ShapeDtypeStruct((k_size, padded), jnp.float32),
        scratch_shapes=[pltpu.VMEM((k_size, k_size + padded), jnp.float32)],
        compiler_params=pltpu.CompilerParams(vmem_limit_bytes=16 * 1024 * 1024),
    )(gram, right_hand)
    return solved[:, :width]


def local(adjusted_rows, base_weight, range_test, corange_test, core_left, core_right):
    highest = lax.Precision.HIGHEST
    f32, bf16 = jnp.float32, jnp.bfloat16
    n_col = lax.axis_size("col")
    rows = adjusted_rows.shape[0]
    width = base_weight.shape[1]
    rank = corange_test.shape[0]
    side = core_left.shape[0]
    step = 128 if rows % 128 == 0 else rows
    left_tests = jnp.concatenate([core_left, corange_test], 0).reshape(side + rank, n_col, rows)
    base_blocks = base_weight.reshape(n_col, rows, width)
    range_parts, left_sum = [], None
    for at in range(0, rows, step):
        block = adjusted_rows[at : at + step].reshape(step, n_col, width).transpose(1, 0, 2)
        block = lax.all_to_all(block, "col", split_axis=0, concat_axis=0, tiled=True)
        difference = (
            block.astype(f32) - base_blocks[:, at : at + step].astype(f32)
        ).astype(bf16).reshape(n_col * step, width)
        tests = left_tests[:, :, at : at + step].reshape(side + rank, n_col * step)
        term = jnp.dot(tests, difference, preferred_element_type=f32)
        left_sum = term if left_sum is None else left_sum + term
        range_parts.append(
            jnp.dot(difference, range_test, preferred_element_type=f32).reshape(n_col, step, rank)
        )
    left_product, corange_part = left_sum[:side], left_sum[side:]
    high = lax.reduce_precision(left_product, 8, 7)
    low = (left_product - high).astype(bf16)
    pieces = jnp.concatenate([high.astype(bf16), low], 0)
    core_two = lax.dot_general(
        core_right, pieces, (((1,), (1,)), ((), ())), preferred_element_type=f32
    )
    projected_two = lax.dot_general(
        range_test, pieces, (((0,), (1,)), ((), ())), preferred_element_type=f32
    )
    share, narrow = side // n_col, rank // n_col
    core_term = (core_two[:, :side] + core_two[:, side:]).reshape(n_col, share, side)
    projected_term = (projected_two[:, :side] + projected_two[:, side:]).reshape(
        n_col, narrow, side
    )
    both = jnp.concatenate([core_term, projected_term], 1)
    both = lax.all_to_all(both, "col", split_axis=0, concat_axis=0, tiled=True).sum(0)
    range_part = jnp.concatenate(range_parts, 1)
    both, range_part = lax.optimization_barrier((both, range_part.astype(bf16)))
    both = lax.psum(both, "row")
    projected = lax.all_gather(both[share:], "col", axis=0, tiled=True)
    projected, corange_part = lax.optimization_barrier((projected, corange_part.astype(bf16)))
    corange_sketch = lax.psum(corange_part, "row").astype(f32)
    range_own = lax.all_to_all(range_part, "col", split_axis=0, concat_axis=0, tiled=True)
    range_own = range_own.astype(f32).sum(0).astype(bf16)
    projected, range_own = lax.optimization_barrier((projected, range_own))
    range_sketch = lax.all_gather(range_own, "col", axis=0, tiled=True).astype(f32)
    gram = jnp.dot(projected, projected.T, precision=highest)
    right_hand = jnp.dot(projected, both[:share].T, precision=highest)
    return (range_sketch, corange_sketch, solve(gram, right_hand))


def solution(mesh):
    in_specs = (
        P(("row", "col"), None),
        P("row", "col"),
        P("col", None),
        P(None, "row"),
        P(None, "row"),
        P(None, "col"),
    )
    out_specs = (P("row", None), P(None, "col"), P(None, "col"))
    return jax.shard_map(local, mesh=mesh, in_specs=in_specs, out_specs=out_specs, check_vma=False)
```
